32 devices in a mesh: tm: 4 (over y, x), atom: 8 (over z, core).
Axes of the slice: x: 2, y: 2, z: 4, core: 2. Of those that a mesh axis runs over, the one named last changes fastest.
Arguments:
- positions: float32 [256, 3, 12288], P('tm', None, 'atom'), may hold values from -0.5 to 1.5, as said below
- species: int32 [12288], P('atom'), may hold values from 0 to 1
- lengths: float32 [2], replicated, may hold values from 0.5 to 2
- wave_numbers: int32 [3, 16], replicated, may hold values from 1 to 16
- lag_list: int32 [128], replicated, may hold values from 0 to 64, as said below
Outputs:
- structure_function: float32 [4096, 128], P('atom')
The draws below stay inside these ranges and needn't reach their ends.
Inputs may be any that keep to these rules, and one draw needn't show every extreme that they name: `positions`: every coordinate lies within the stated bounds. `lag_list`: the first entry is 64; lags may repeat.
All inputs are finite; a program needn't handle non-finite values.
Results may differ from the reference program's by a relative error of at most 0.00043.
Values sent between devices are 32-bit elements; how exact they have to be, the bound alone decides.
No kernel may reach another device: no remote copies, remote signals or barrier semaphores. Data moves between devices by JAX's collectives and lax.ppermute only.
A program may use at most 64 MiB of HBM per device.

```python
import math
import jax
import jax.numpy as jnp
from jax import lax

NQ = 16
SPECIES = 2
NLAG = 128
FRAMES = 256
ATOMS = 12288
MAXLAG = 64


def draw_positions(key, part):
    key = jax.random.fold_in(key, 11)
    key_base, key_vel, key_jit = jax.random.split(key, 3)
    base = jax.random.uniform(key_base, (3, ATOMS), jnp.float32)
    velocity = jnp.clip(jax.random.normal(key_vel, (3, ATOMS), jnp.float32), -3.0, 3.0)
    jitter = jnp.clip(jax.random.normal(key_jit, (FRAMES, 3, ATOMS), jnp.float32), -4.0, 4.0) * 0.005
    times = jnp.arange(FRAMES, dtype=jnp.float32) * (0.03 / MAXLAG)
    return base[None, :, :] + velocity[None, :, :] * times[:, None, None] + jitter


def draw_lag_list(key, part):
    key = jax.random.fold_in(key, 5)
    lags = jax.random.randint(key, (NLAG,), 0, MAXLAG + 1, jnp.int32)
    return lags.at[0].set(MAXLAG)


def set_ends(array, rng, smallest, largest):
    longest = array.shape.index(max(array.shape))
    spots = []
    for shift in (0, 1):
        where = [jax.random.randint(jax.random.fold_in(rng, axis), (), 0, length) for axis, length in enumerate(array.shape)]
        where[longest] = (where[longest] + shift) % array.shape[longest]
        spots.append(tuple(where))
    return array.at[spots[0]].set(smallest).at[spots[1]].set(largest)


def setup_inputs(seed: int = 0) -> dict:
    streams_of = jax.random.split(jax.random.key(seed), 6)
    return {
        "positions": draw_positions(jax.random.fold_in(streams_of[5], 71), 0),
        "species": set_ends(jax.random.randint(streams_of[1], (ATOMS,), 0, SPECIES), jax.random.fold_in(streams_of[1], 1), 0, SPECIES - 1).astype(jnp.int32),
        "lengths": jnp.clip(jax.random.uniform(streams_of[2], (SPECIES,), jnp.float32, 0.5, 2.0), 0.5, 2.0),
        "wave_numbers": set_ends(jax.random.randint(streams_of[3], (3, NQ), 1, 17), jax.random.fold_in(streams_of[3], 1), 1, 16).astype(jnp.int32),
        "lag_list": draw_lag_list(jax.random.fold_in(streams_of[5], 71), 0),
    }


TWO_PI = 2.0 * math.pi


def atom_weight(species, lengths):
    labels = jnp.arange(lengths.shape[0], dtype=jnp.int32)
    return jnp.sum(jnp.where(species[None, :] == labels[:, None], lengths[:, None], 0.0), axis=0)


def frame_density(frame, weight, scaled):
    angle = scaled[:, :, None] * frame[:, None, :]
    cosine = jnp.cos(angle)
    sine = jnp.sin(angle)
    real = cosine[0][:, None, :] * cosine[1][None, :, :] - sine[0][:, None, :] * sine[1][None, :, :]
    imag = cosine[0][:, None, :] * sine[1][None, :, :] + sine[0][:, None, :] * cosine[1][None, :, :]
    pairs = NQ * NQ
    left = jnp.concatenate([real.reshape(pairs, -1), imag.reshape(pairs, -1)], axis=0).astype(jnp.bfloat16)
    right = jnp.concatenate([weight[None, :] * cosine[2], weight[None, :] * sine[2]], axis=0).astype(jnp.bfloat16)
    prod = jnp.dot(left, right.T, preferred_element_type=jnp.float32)
    rho_re = prod[:pairs, :NQ] - prod[pairs:, NQ:]
    rho_im = prod[:pairs, NQ:] + prod[pairs:, :NQ]
    return rho_re.reshape(-1), rho_im.reshape(-1)


def reference(positions, species, lengths, wave_numbers, lag_list):
    weight = atom_weight(species, lengths)
    scaled = TWO_PI * wave_numbers.astype(jnp.float32)
    rho_re, rho_im = lax.map(lambda frame: frame_density(frame, weight, scaled), positions)
    zeros_pad = jnp.zeros((MAXLAG, rho_re.shape[1]), rho_re.dtype)
    pad_re = jnp.concatenate([rho_re, zeros_pad], axis=0)
    pad_im = jnp.concatenate([rho_im, zeros_pad], axis=0)

    def one_lag(lag):
        later_re = lax.dynamic_slice_in_dim(pad_re, lag.astype(jnp.int32), FRAMES, 0)
        later_im = lax.dynamic_slice_in_dim(pad_im, lag.astype(jnp.int32), FRAMES, 0)
        total = jnp.sum(later_re * rho_re + later_im * rho_im, axis=0)
        return total / ((FRAMES - lag).astype(jnp.float32) * ATOMS)

    return lax.map(one_lag, lag_list).T
```

```python
import functools
import math

import jax
import jax.numpy as jnp
import numpy as np
from jax import lax
from jax.experimental import pallas as pl
from jax.experimental.pallas import tpu as pltpu
from jax.sharding import PartitionSpec as P

COS = (1.0, -19.73920440673828, 64.93911743164062, -85.45014190673828, 60.16762924194336, -25.967599868774414, 6.528658390045166)
SIN = (6.2831854820251465, -41.34170150756836, 81.60513305664062, -76.70301818847656, 42.02592849731445, -14.899847030639648, 3.2381374835968018)

CHUNKS = 2
PITCH = 17
WIDE = 33
VMEM_LIMIT = 48 << 20


def polynomial(coefficients, s):
    value = coefficients[-1] * s + coefficients[-2]
    for c in coefficients[-3::-1]:
        value = value * s + c
    return value


def circle(turns):
    r = turns - jnp.round(turns)
    s = r * r
    return polynomial(COS, s), polynomial(SIN, s) * r


def tables(x, y, z, weight, put_x, put_y, put_z):
    c, s = circle(0.5 * x)
    twice = 4.0 * c * c - 2.0
    cs = [c, (twice - 1.0) * c]
    ss = [s, (twice + 1.0) * s]
    for _ in range(6):
        cs.append(twice * cs[-1] - cs[-2])
        ss.append(twice * ss[-1] - ss[-2])
    for m in range(8):
        put_x(m, cs[m])
        put_x(8 + m, ss[m])
    c, s = circle(0.5 * y)
    twice = 4.0 * c * c - 2.0
    for l, value in enumerate((c, s, (twice - 1.0) * c, (twice + 1.0) * s)):
        put_y(l, value)
    c2 = 0.5 * twice * twice - 1.0
    s2 = 2.0 * twice * s * c
    four = 4.0 * c2 * c2
    for h, value in enumerate((c2, s2, c2 * (four - 3.0), s2 * (four - 1.0))):
        put_y(4 + h, value)
    real, imag = circle(8.5 * (x + y))
    c, s = circle(z)
    twice = c + c
    cs = [c, twice * c - 1.0]
    ss = [s, twice * s]
    for _ in range(14):
        cs.append(twice * cs[-1] - cs[-2])
        ss.append(twice * ss[-1] - ss[-2])
    for k in range(16):
        c = (weight * cs[k]).astype(jnp.bfloat16).astype(jnp.float32)
        s = (weight * ss[k]).astype(jnp.bfloat16).astype(jnp.float32)
        put_z(k, real * c - imag * s)
        put_z(16 + k, real * s + imag * c)


def split(value):
    high = value.astype(jnp.bfloat16)
    return high, (value - high.astype(jnp.float32)).astype(jnp.bfloat16)


def slot_of(k):
    return jnp.where(k >= 9, k - 9, 16 - k)


def turned(value, quarter):
    return pltpu.roll(value, 64, 1) * quarter


def density_kernel(me_ref, wave_ref, own_ref, sibling_ref, keep_ref, send_ref, xs, ys, zs, prod, grid, *, first, bits, shift):
    sources = (own_ref, sibling_ref)
    rows = (own_ref.shape[0] - 8) // 3
    tiles = own_ref.shape[1] // 128
    base = pl.multiple_of((first + pl.program_id(0)) * 8, 8)
    for i, source in enumerate(sources):

        def one_tile(j, carry):
            lanes = pl.ds(pl.multiple_of(j * 128, 128), 128)
            x = source[pl.ds(base, 8), lanes]
            y = source[pl.ds(base + rows, 8), lanes]
            z = source[pl.ds(base + 2 * rows, 8), lanes]
            weight = source[pl.ds(3 * rows, 8), lanes]

            def put(ref, pitch):
                def go(f, value):
                    ref[i * tiles + j, pl.ds(f, 8, stride=pitch), :] = value

                return go

            tables(x, y, z, weight, put(xs, PITCH), put(ys, PITCH), put(zs, WIDE))
            return carry

        lax.fori_loop(0, tiles, one_tile, 0, unroll=2)

    def one_frame(f, carry):
        r0 = f * PITCH
        total = jnp.zeros((128, 128), jnp.float32)
        for pair in range(len(sources) * tiles // 2):
            left, right = [], []
            for t in (2 * pair, 2 * pair + 1):
                x = xs[t, pl.ds(r0, 16), :]
                z = zs[t, pl.ds(f * WIDE, 32), :]
                exact = jnp.concatenate([x * ys[t, pl.ds(r0 + l, 1), :] for l in range(4)], 0)
                left.append(jnp.concatenate(split(exact), 0))
                hs = [ys[t, pl.ds(r0 + 4 + h, 1), :] for h in range(4)]
                right.append(jnp.concatenate([part * h for part in (z[:16], z[16:]) for h in hs], 0).astype(jnp.bfloat16))
            total = total + lax.dot_general(
                jnp.concatenate(left, 1),
                jnp.concatenate(right, 1),
                (((1,), (1,)), ((), ())),
                preferred_element_type=jnp.float32,
            )
        prod[f] = total[:64] + total[64:]
        return carry

    lax.fori_loop(0, 8, one_frame, 0, unroll=8)

    lane = lax.broadcasted_iota(jnp.int32, (8, 128), 1)
    quarter = jnp.where(lane < 64, -1.0, 1.0).astype(jnp.float32)
    for f in range(8):
        for l in range(4):
            cosine = prod[f, l * 16 : l * 16 + 8, :]
            sine = turned(prod[f, l * 16 + 8 : l * 16 + 16, :], quarter)
            r = (f * 4 + l) * PITCH
            grid[r : r + 8, :] = cosine + sine
            grid[r + 8 : r + 16, :] = cosine - sine

    me = me_ref[0]
    for i in range(8):
        flip = sum(((i >> (2 - j)) & 1) << bit for j, bit in enumerate(bits))
        pair = (me ^ flip) >> shift
        out_ref = keep_ref if i < 4 else send_ref
        for j in range(2):
            slot = slot_of(wave_ref[0, 2 * pair + j])
            for f in range(8):
                out_ref[f, i % 4, 4 * j : 4 * j + 4, :] = grid[pl.ds(f * 4 * PITCH + slot, 4, stride=PITCH), :]


def density(me, wave_numbers, own, sibling, first, groups, bits, shift):
    tiles = 2 * own.shape[1] // 128
    table = pltpu.VMEM((tiles, 8 * PITCH, 128), jnp.float32)
    block = pl.BlockSpec((8, 4, 8, 128), lambda g: (g, 0, 0, 0))
    shape = jax.ShapeDtypeStruct((groups * 8, 4, 8, 128), jnp.float32)
    frames = groups * 8
    return pl.pallas_call(
        functools.partial(density_kernel, first=first, bits=bits, shift=shift),
        grid=(groups,),
        out_shape=(shape, shape),
        in_specs=[pl.BlockSpec(memory_space=pltpu.SMEM)] * 2 + [pl.BlockSpec(own.shape, lambda g: (0, 0))] * 2,
        out_specs=(block, block),
        scratch_shapes=[
            table,
            table,
            pltpu.VMEM((tiles, 8 * WIDE, 128), jnp.float32),
            pltpu.VMEM((8, 64, 128), jnp.float32),
            pltpu.VMEM((32 * PITCH, 128), jnp.float32),
        ],
        compiler_params=pltpu.CompilerParams(vmem_limit_bytes=VMEM_LIMIT),
        cost_estimate=pl.CostEstimate(flops=frames * tiles * 128 * 64 * 128 * 2 * 8, bytes_accessed=frames * 32768, transcendentals=0),
        name="density",
    )(me, wave_numbers, own, sibling)


def combine(value, swap, second, quarter):
    mixed = jnp.where(second, turned(value, quarter), value)
    return swap(mixed) + jnp.where(second, -mixed, mixed)


def waves_kernel(*refs, terms):
    parts, outs = refs[:terms], refs[terms:]
    frames = parts[0].shape[0]
    row = lax.broadcasted_iota(jnp.int32, (8, 128), 0)
    lane = lax.broadcasted_iota(jnp.int32, (8, 128), 1)
    quarter = jnp.where(lane < 64, -1.0, 1.0).astype(jnp.float32)
    bit_l, bit_h = (row & 1) == 1, (lane & 16) == 16

    def swap(axis, distance, second):
        size = (8, 128)[axis]

        def go(value):
            return jnp.where(second, pltpu.roll(value, distance, axis), pltpu.roll(value, size - distance, axis))

        return go

    for g, out in enumerate(outs):
        for t in range(frames):
            value = parts[0][t, g]
            for part in parts[1:]:
                value = value + part[t, g]
            value = combine(value, swap(0, 1, bit_l), bit_l, quarter)
            value = combine(value, swap(1, 16, bit_h), bit_h, quarter)
            out[:, t, :] = value


def waves(parts, groups):
    frames = parts[0].shape[0]
    shape = jax.ShapeDtypeStruct((8, frames, 128), jnp.float32)
    return pl.pallas_call(
        functools.partial(waves_kernel, terms=len(parts)),
        grid=(1,),
        out_shape=(shape,) * groups,
        in_specs=[pl.BlockSpec((frames, groups, 8, 128), lambda g: (0, 0, 0, 0))] * len(parts),
        out_specs=(pl.BlockSpec((8, frames, 128), lambda g: (0, 0, 0)),) * groups,
        compiler_params=pltpu.CompilerParams(vmem_limit_bytes=VMEM_LIMIT),
        name="waves",
    )(*parts)


def lags_kernel(place_ref, wave_ref, lag_ref, basis_ref, *refs, blocks, frames, atoms, period, share):
    parts, (out_ref, series, result) = refs[:blocks], refs[blocks:]
    half = period // 2
    tm, me = place_ref[0], place_ref[1]
    chunk = parts[0].shape[2]
    steps = blocks // CHUNKS
    per_block = frames // steps
    for p in range(steps):
        for c in range(CHUNKS):
            for side in range(2):
                core = (me & 1) ^ side
                start = (tm ^ p) * per_block + core * (per_block // 2) + c * chunk
                series[:, pl.ds(pl.multiple_of(start, chunk), chunk), :] = parts[p * CHUNKS + c][side]
    lane = lax.broadcasted_iota(jnp.int32, (8, 128), 1)
    source = lane
    for n in range(16):
        source = jnp.where((lane & 15) == n, lane - n + wave_ref[2, n] - 1, source)
    order = 2 * lax.broadcasted_iota(jnp.int32, (half, 128), 0) + 1
    lag = lag_ref[...]
    phase = (order * lag).astype(jnp.float32)
    turns = phase - jnp.round(phase * (0.5 / period)) * (2.0 * period)
    cosine, _ = circle(turns * (0.5 / period))
    scale = (2.0 / period) / ((frames - lag).astype(jnp.float32) * float(atoms))
    cosine = cosine * scale
    for l in range(4):
        powers = []
        for a in range(2):
            high, low = split(series[4 * a + l])
            spectrum = jnp.dot(basis_ref[...], jnp.concatenate([high, high, low], 0), preferred_element_type=jnp.float32)
            power = spectrum[:half] * spectrum[:half] + spectrum[half:] * spectrum[half:]
            powers.append(power + pltpu.roll(power, 64, 1))
        power = jnp.concatenate(
            [
                jnp.take_along_axis(jnp.where(lane < 64, powers[0][i : i + 8], powers[1][i : i + 8]), source, axis=1)
                for i in range(0, half, 8)
            ],
            0,
        )
        result[l] = jnp.dot(power.T, cosine, precision=lax.Precision.HIGHEST, preferred_element_type=jnp.float32)
    for i in range(share // 16):
        block = (me * (share // 16) + i) % 32
        k = wave_ref[1, block % 16] - 1
        hi, lo = k // 4, k % 4
        slot = [jnp.where(v == 0, 3, jnp.where(v == 1, 1, jnp.where(v == 2, 0, 2))) for v in (hi, lo)]
        start = pl.multiple_of((block // 16) * 64 + slot[0] * 16, 16)
        out_ref[i * 16 : i * 16 + 16, :] = result[slot[1], pl.ds(start, 16), :]


def lags(place, wave_numbers, lag_list, parts, frames, atoms, period, share):
    half = period // 2
    angle = np.outer(2 * np.arange(half) + 1, np.arange(frames)) * (math.pi / period)
    basis = np.concatenate([np.cos(angle), np.sin(angle)], 0).astype(np.float32)
    high = basis.astype(jnp.bfloat16)
    low = (basis - high.astype(np.float32)).astype(jnp.bfloat16)
    basis = jnp.asarray(np.concatenate([high, low, high], 1))
    smem = pl.BlockSpec(memory_space=pltpu.SMEM)
    vmem = pl.BlockSpec(memory_space=pltpu.VMEM)
    return pl.pallas_call(
        functools.partial(lags_kernel, blocks=len(parts), frames=frames, atoms=atoms, period=period, share=share),
        out_shape=jax.ShapeDtypeStruct((share, lag_list.shape[0]), jnp.float32),
        in_specs=[smem, smem] + [vmem] * (2 + len(parts)),
        out_specs=vmem,
        scratch_shapes=[pltpu.VMEM((8, frames, 128), jnp.float32), pltpu.VMEM((4, 128, lag_list.shape[0]), jnp.float32)],
        compiler_params=pltpu.CompilerParams(vmem_limit_bytes=VMEM_LIMIT),
        name="lags",
    )(place, wave_numbers, lag_list[None, :], basis, *parts)


def swapped(block, axis, flip):
    return lax.ppermute(block, axis, [(i, i ^ flip) for i in range(lax.axis_size(axis))])


def on_device(positions, species, lengths, wave_numbers, lag_list):
    frames, _, atoms = positions.shape
    devices, blocks = lax.axis_size("atom"), lax.axis_size("tm")
    me, tm = lax.axis_index("atom"), lax.axis_index("tm")
    share = wave_numbers.shape[1] ** 3 // devices
    period = (frames * blocks * 5) // 4
    half = frames // 2
    shift = devices.bit_length() - 4
    flips = [1 << bit for bit in range(1, devices.bit_length() - 1)]
    bits = ([bit for bit in range(1, devices.bit_length() - 1) if bit >= shift] + [0])[:3]

    labels = jnp.arange(lengths.shape[0], dtype=jnp.int32)
    weight = jnp.sum(jnp.where(species[None, :] == labels[:, None], lengths[:, None], 0.0), axis=0)
    turned = jnp.transpose(positions, (1, 0, 2))

    def payload(core):
        part = lax.dynamic_slice_in_dim(turned, core * half, half, 1).reshape(3 * half, atoms)
        return jnp.concatenate([part, jnp.broadcast_to(weight[None, :], (8, atoms))], 0)

    own = payload(me & 1)
    sibling = swapped(payload(1 - (me & 1)), "atom", 1)
    place = jnp.stack([tm, me]).astype(jnp.int32)

    groups = half // 8 // CHUNKS
    parts = [[None] * CHUNKS for _ in range(blocks)]
    for c in range(CHUNKS):
        keep, send = density(place[1:2], wave_numbers, own, sibling, c * groups, groups, bits, shift)
        terms, fresh, held = [keep], True, 8
        for flip in flips:
            if flip >= (1 << shift):
                held //= 2
                out = send if fresh else sum(t[:, held : 2 * held] for t in terms)
                fresh = False
                terms = terms + [swapped(out, "atom", flip)]
            else:
                keep, send = (a + swapped(a, "atom", flip) for a in (keep, send))
                terms = [keep]
        final = waves(terms, held)
        mine, other = final[0], final[-1]
        both = jnp.stack([mine, swapped(other, "atom", 1)])
        for p in range(blocks):
            parts[p][c] = both if p == 0 else swapped(both, "tm", p)
    parts = [part for row in parts for part in row]
    return lags(place, wave_numbers, lag_list, parts, frames * blocks, atoms * devices, period, share)


def solution(mesh):
    placed = (P("tm", None, "atom"), P("atom"), P(), P(), P())
    return jax.shard_map(
        on_device, mesh=mesh, in_specs=placed, out_specs=P("atom", None), check_vma=False
    )
```

```python
import functools
import math

import jax
import jax.numpy as jnp
import numpy as np
from jax import lax
from jax.experimental import pallas as pl
from jax.experimental.pallas import tpu as pltpu
from jax.sharding import PartitionSpec as P

COS = (1.0, -19.73920440673828, 64.93911743164062, -85.45014190673828, 60.16762924194336, -25.967599868774414, 6.528658390045166)
SIN = (6.2831854820251465, -41.34170150756836, 81.60513305664062, -76.70301818847656, 42.02592849731445, -14.899847030639648, 3.2381374835968018)

SIZES = (2, 1, 1)
RINGS = ((0,), (1, 2))
TIES = ((2, 0),)
PITCH = 17
WIDE = 33
VMEM_LIMIT = 48 << 20


def polynomial(coefficients, s):
    value = coefficients[-1] * s + coefficients[-2]
    for c in coefficients[-3::-1]:
        value = value * s + c
    return value


def circle(turns):
    r = turns - jnp.round(turns)
    s = r * r
    return polynomial(COS, s), polynomial(SIN, s) * r


def tables(x, y, z, weight, put_x, put_y, put_z):
    c, s = circle(0.5 * x)
    twice = 4.0 * c * c - 2.0
    before, now = (c, -s), (c, s)
    for m in range(8):
        put_x(m, now[0])
        put_x(8 + m, now[1])
        before, now = now, tuple(twice * p - q for p, q in zip(now, before))
    c, s = circle(0.5 * y)
    twice = 4.0 * c * c - 2.0
    for l, value in enumerate((c, s, (twice - 1.0) * c, (twice + 1.0) * s)):
        put_y(l, value)
    c2 = 0.5 * twice * twice - 1.0
    s2 = 2.0 * twice * s * c
    four = 4.0 * c2 * c2
    for h, value in enumerate((c2, s2, c2 * (four - 3.0), s2 * (four - 1.0))):
        put_y(4 + h, value)
    real, imag = circle(8.5 * (x + y))
    c, s = circle(z)
    twice = c + c
    before, now = (weight, jnp.zeros_like(weight)), (weight * c, weight * s)
    for k in range(16):
        c, s = (value.astype(jnp.bfloat16).astype(jnp.float32) for value in now)
        put_z(k, real * c - imag * s)
        put_z(16 + k, real * s + imag * c)
        before, now = now, tuple(twice * p - q for p, q in zip(now, before))


def split(value):
    high = value.astype(jnp.bfloat16)
    return high, (value - high.astype(jnp.float32)).astype(jnp.bfloat16)


def slot_of(k):
    return jnp.where(k >= 9, k - 9, 16 - k)


def turned(value, quarter):
    return pltpu.roll(value, 64, 1) * quarter


def density_kernel(
    me_ref, wave_ref, length_ref, own_ref, sibling_ref, own_label, sibling_label, keep_ref, send_ref, *scratch, groups, bits, shift
):
    xs, ys, zs, prod, grid = scratch
    sources = ((own_ref, own_label), (sibling_ref, sibling_label))
    rows = own_ref.shape[0] // 3
    tiles = own_ref.shape[1] // 128

    def fill(g, source, j):
        ref, label_ref = sources[source]
        base = pl.multiple_of(g * 8, 8)
        lanes = pl.ds(pl.multiple_of(j * 128, 128), 128)
        x, y, z = (ref[pl.ds(base + rows * axis, 8), lanes] for axis in range(3))
        label = jnp.broadcast_to(label_ref[:, lanes], (8, 128))
        weight = jnp.zeros((8, 128), jnp.float32)
        for kind in range(length_ref.shape[0]):
            weight = weight + jnp.where(label == kind, length_ref[kind], 0.0)

        def put(table, pitch):
            def go(f, value):
                table[source * tiles + j, pl.ds(f, 8, stride=pitch), :] = value

            return go

        tables(x, y, z, weight, put(xs, PITCH), put(ys, PITCH), put(zs, WIDE))

    def one_frame(f, carry):
        r0 = f * PITCH
        total = jnp.zeros((128, 128), jnp.float32)
        for pair in range(tiles):
            left, right = [], []
            for t in (2 * pair, 2 * pair + 1):
                x = xs[t, pl.ds(r0, 16), :]
                z = zs[t, pl.ds(f * WIDE, 32), :]
                exact = jnp.concatenate([x * ys[t, pl.ds(r0 + l, 1), :] for l in range(4)], 0)
                left.append(jnp.concatenate(split(exact), 0))
                hs = [ys[t, pl.ds(r0 + 4 + h, 1), :] for h in range(4)]
                right.append(jnp.concatenate([part * h for part in (z[:16], z[16:]) for h in hs], 0).astype(jnp.bfloat16))
            total = total + lax.dot_general(
                jnp.concatenate(left, 1),
                jnp.concatenate(right, 1),
                (((1,), (1,)), ((), ())),
                preferred_element_type=jnp.float32,
            )
        prod[f] = total[:64] + total[64:]
        return carry

    def one_group(g, carry):
        for source in range(2):

            def one_tile(j, carry):
                fill(g, source, j)
                return carry

            lax.fori_loop(0, tiles, one_tile, 0, unroll=4)
        lax.fori_loop(0, 8, one_frame, 0, unroll=8)
        collect(g, me_ref, wave_ref, keep_ref, send_ref, prod, grid, bits, shift)
        return carry

    lax.fori_loop(0, groups, one_group, 0)


def collect(g, me_ref, wave_ref, keep_ref, send_ref, prod, grid, bits, shift):
    lane = lax.broadcasted_iota(jnp.int32, (8, 128), 1)
    quarter = jnp.where(lane < 64, -1.0, 1.0).astype(jnp.float32)
    for f in range(8):
        for l in range(4):
            cosine = prod[f, l * 16 : l * 16 + 8, :]
            sine = turned(prod[f, l * 16 + 8 : l * 16 + 16, :], quarter)
            r = (f * 4 + l) * PITCH
            grid[r : r + 8, :] = cosine + sine
            grid[r + 8 : r + 16, :] = cosine - sine

    me = me_ref[0]
    for i in range(8):
        flip = sum(((i >> (2 - j)) & 1) << bit for j, bit in enumerate(bits))
        pair = (me ^ flip) >> shift
        out_ref = keep_ref if i < 4 else send_ref
        for j in range(2):
            slot = slot_of(wave_ref[0, 2 * pair + j])
            for f in range(8):
                out_ref[g * 8 + f, i % 4, 4 * j : 4 * j + 4, :] = grid[pl.ds(f * 4 * PITCH + slot, 4, stride=PITCH), :]


def density(me, wave_numbers, lengths, own, sibling, own_label, sibling_label, groups, bits, shift):
    tiles = own.shape[1] // 128
    frames = groups * 8
    shape = jax.ShapeDtypeStruct((frames, 4, 8, 128), jnp.float32)
    smem, vmem = (pl.BlockSpec(memory_space=space) for space in (pltpu.SMEM, pltpu.VMEM))
    tables_shapes = [pltpu.VMEM((2 * tiles, 8 * pitch, 128), jnp.float32) for pitch in (PITCH, PITCH, WIDE)]
    return pl.pallas_call(
        functools.partial(density_kernel, groups=groups, bits=bits, shift=shift),
        out_shape=(shape, shape),
        in_specs=[smem] * 3 + [vmem] * 4,
        out_specs=(vmem, vmem),
        scratch_shapes=tables_shapes + [pltpu.VMEM((8, 64, 128), jnp.float32), pltpu.VMEM((32 * PITCH, 128), jnp.float32)],
        compiler_params=pltpu.CompilerParams(vmem_limit_bytes=VMEM_LIMIT),
        cost_estimate=pl.CostEstimate(flops=frames * tiles * 128 * 128 * 128 * 2 * 8, bytes_accessed=frames * 32768, transcendentals=0),
        name="density",
    )(me, wave_numbers, lengths, own, sibling, own_label, sibling_label)


def combine(value, swap, second, quarter):
    mixed = jnp.where(second, turned(value, quarter), value)
    return swap(mixed) + jnp.where(second, -mixed, mixed)


def waves_kernel(*refs, terms):
    parts, outs = refs[:terms], refs[terms:]
    frames = parts[0].shape[0]
    row = lax.broadcasted_iota(jnp.int32, (8, 128), 0)
    lane = lax.broadcasted_iota(jnp.int32, (8, 128), 1)
    quarter = jnp.where(lane < 64, -1.0, 1.0).astype(jnp.float32)
    bit_l, bit_h = (row & 1) == 1, (lane & 16) == 16

    def swap(axis, distance, second):
        size = (8, 128)[axis]

        def go(value):
            return jnp.where(second, pltpu.roll(value, distance, axis), pltpu.roll(value, size - distance, axis))

        return go

    for g, out in enumerate(outs):
        for t in range(frames):
            value = parts[0][t, g]
            for part in parts[1:]:
                value = value + part[t, g]
            value = combine(value, swap(0, 1, bit_l), bit_l, quarter)
            value = combine(value, swap(1, 16, bit_h), bit_h, quarter)
            out[:, t, :] = value


def waves(parts, groups):
    frames = parts[0].shape[0]
    shape = jax.ShapeDtypeStruct((8, frames, 128), jnp.float32)
    return pl.pallas_call(
        functools.partial(waves_kernel, terms=len(parts)),
        grid=(1,),
        out_shape=(shape,) * groups,
        in_specs=[pl.BlockSpec((frames, groups, 8, 128), lambda g: (0, 0, 0, 0))] * len(parts),
        out_specs=(pl.BlockSpec((8, frames, 128), lambda g: (0, 0, 0)),) * groups,
        compiler_params=pltpu.CompilerParams(vmem_limit_bytes=VMEM_LIMIT),
        name="waves",
    )(*parts)


def lags_kernel(place_ref, wave_ref, lag_ref, basis_ref, *refs, blocks, frames, atoms, period, share):
    parts, (out_ref, series, result) = refs[:blocks], refs[blocks:]
    half = period // 2
    tm, me = place_ref[0], place_ref[1]
    steps = blocks // len(RINGS)
    per_block = frames // steps
    at = 0
    for ring in range(len(RINGS)):
        size = parts[ring * steps].shape[2]
        for p in range(steps):
            for side in range(2):
                start = (tm ^ p) * per_block + ((me & 1) ^ side) * (per_block // 2) + at
                series[:, pl.ds(pl.multiple_of(start, 8), size), :] = parts[ring * steps + p][side]
        at += size
    lane = lax.broadcasted_iota(jnp.int32, (8, 128), 1)
    source = lane
    for n in range(16):
        source = jnp.where((lane & 15) == n, lane - n + wave_ref[2, n] - 1, source)
    count = lag_ref.shape[1]
    order = 2 * lax.broadcasted_iota(jnp.int32, (count, half), 1) + 1
    lag = jnp.broadcast_to(lag_ref[...], (half, count)).T
    phase = (order * lag).astype(jnp.float32)
    turns = phase - jnp.round(phase * (0.5 / period)) * (2.0 * period)
    cosine, _ = circle(turns * (0.5 / period))
    scale = (2.0 / period) / ((frames - lag).astype(jnp.float32) * float(atoms))
    high, low = split(cosine * scale)
    weights = jnp.concatenate([high, low, high], 1)
    powers = []
    for l in range(4):
        high, low = split(jnp.concatenate([series[l], series[4 + l]], 1))
        spectrum = jnp.dot(basis_ref[...], jnp.concatenate([high, high, low], 0), preferred_element_type=jnp.float32)
        power = spectrum[:half] * spectrum[:half] + spectrum[half:] * spectrum[half:]
        powers.append(
            jnp.concatenate(
                [
                    jnp.where(
                        lane < 64,
                        power[i : i + 8, :128] + pltpu.roll(power[i : i + 8, :128], 64, 1),
                        power[i : i + 8, 128:] + pltpu.roll(power[i : i + 8, 128:], 64, 1),
                    )
                    for i in range(0, half, 8)
                ],
                0,
            )
        )
    high, low = split(jnp.concatenate(powers, 1))
    total = jnp.dot(weights, jnp.concatenate([high, high, low], 0), preferred_element_type=jnp.float32)
    for l in range(4):
        part = total[:, l * 128 : l * 128 + 128]
        part = jnp.concatenate([jnp.take_along_axis(part[i : i + 8], source, axis=1) for i in range(0, count, 8)], 0)
        result[l] = part.T

    def place_of(b):
        k = wave_ref[1, b] - 1
        h, l = (jnp.where(v == 0, 3, jnp.where(v == 1, 1, jnp.where(v == 2, 0, 2))) for v in (k // 4, k % 4))
        return l, h * 16

    rows = share // 16
    known = [place_of(b) for b in range(16)] if rows == 32 else None
    for i in range(rows):
        if known:
            a, (l, start) = i // 16, known[i % 16]
        else:
            block = (me * rows + i) % 32
            a, (l, start) = block // 16, place_of(block % 16)
        out_ref[i * 16 : i * 16 + 16, :] = result[l, pl.ds(pl.multiple_of(a * 64 + start, 16), 16), :]


def lags(place, wave_numbers, lag_list, parts, frames, atoms, period, share):
    half = period // 2
    angle = np.outer(2 * np.arange(half) + 1, np.arange(frames)) * (math.pi / period)
    basis = np.concatenate([np.cos(angle), np.sin(angle)], 0).astype(np.float32)
    high = basis.astype(jnp.bfloat16)
    low = (basis - high.astype(np.float32)).astype(jnp.bfloat16)
    basis = jnp.asarray(np.concatenate([high, low, high], 1))
    smem = pl.BlockSpec(memory_space=pltpu.SMEM)
    vmem = pl.BlockSpec(memory_space=pltpu.VMEM)
    return pl.pallas_call(
        functools.partial(lags_kernel, blocks=len(parts), frames=frames, atoms=atoms, period=period, share=share),
        out_shape=jax.ShapeDtypeStruct((share, lag_list.shape[0]), jnp.float32),
        in_specs=[smem, smem] + [vmem] * (2 + len(parts)),
        out_specs=vmem,
        scratch_shapes=[pltpu.VMEM((8, frames, 128), jnp.float32), pltpu.VMEM((4, 128, lag_list.shape[0]), jnp.float32)],
        compiler_params=pltpu.CompilerParams(vmem_limit_bytes=VMEM_LIMIT),
        name="lags",
    )(place, wave_numbers, lag_list[None, :], basis, *parts)


def swapped(block, axis, flip):
    return lax.ppermute(block, axis, [(i, i ^ flip) for i in range(lax.axis_size(axis))])


def on_device(positions, species, lengths, wave_numbers, lag_list):
    frames, _, atoms = positions.shape
    devices, blocks = lax.axis_size("atom"), lax.axis_size("tm")
    me, tm = lax.axis_index("atom"), lax.axis_index("tm")
    share = wave_numbers.shape[1] ** 3 // devices
    period = (frames * blocks * 5) // 4
    half = frames // 2
    shift = devices.bit_length() - 4
    flips = [1 << bit for bit in range(1, devices.bit_length() - 1)]
    bits = ([bit for bit in range(1, devices.bit_length() - 1) if bit >= shift] + [0])[:3]

    turned_positions = jnp.transpose(positions, (1, 0, 2))
    sizes = [size * 8 for size in SIZES]

    def payload(core, start, size):
        part = lax.dynamic_slice_in_dim(turned_positions, core * half + start, size, 1)
        return part.reshape(3 * size, atoms)

    labels = [species[None, :], swapped(species, "atom", 1)[None, :]]
    place = jnp.stack([tm, me]).astype(jnp.int32)
    finals, rings = [], []
    for c, size in enumerate(sizes):
        start = sum(sizes[:c])
        own = payload(me & 1, start, size)
        sibling = swapped(payload(1 - (me & 1), start, size), "atom", 1)
        keep, send = density(place[1:2], wave_numbers, lengths, own, sibling, *labels, size // 8, bits, shift)
        terms, fresh, held = [keep], True, 8
        for flip in flips:
            if flip >= (1 << shift):
                held //= 2
                out = send if fresh else sum(t[:, held : 2 * held] for t in terms)
                fresh = False
                terms = terms + [swapped(out, "atom", flip)]
            else:
                keep, send = (a + swapped(a, "atom", flip) for a in (keep, send))
                terms = [keep]
        for chunk, ring in TIES:
            if chunk == c:
                terms[-1], *rings[ring][1:] = lax.optimization_barrier((terms[-1], *rings[ring][1:]))
        final = waves(terms, held)
        finals.append((final[0], final[-1]))
        for ring in RINGS:
            if ring[-1] == c:
                mine, other = (jnp.concatenate([finals[i][j] for i in ring], 1) for j in range(2))
                both = jnp.stack([mine, swapped(other, "atom", 1)])
                rings.append([both] + [swapped(both, "tm", p) for p in range(1, blocks)])
    parts = [part for ring in rings for part in ring]
    return lags(place, wave_numbers, lag_list, parts, frames * blocks, atoms * devices, period, share)


def solution(mesh):
    placed = (P("tm", None, "atom"), P("atom"), P(), P(), P())
    return jax.shard_map(
        on_device, mesh=mesh, in_specs=placed, out_specs=P("atom", None), check_vma=False
    )
```

```python
import functools
import math

import jax
import jax.numpy as jnp
import numpy as np
from jax import lax
from jax.experimental import pallas as pl
from jax.experimental.pallas import tpu as pltpu
from jax.sharding import PartitionSpec as P

COS = (1.0, -19.73920440673828, 64.93911743164062, -85.45014190673828, 60.16762924194336, -25.967599868774414, 6.528658390045166)
SIN = (6.2831854820251465, -41.34170150756836, 81.60513305664062, -76.70301818847656, 42.02592849731445, -14.899847030639648, 3.2381374835968018)

SIZES = (2, 1, 1)
RINGS = ((0,), (1, 2))
TIES = ((2, 0),)
PITCH = 17
WIDE = 33
VMEM_LIMIT = 48 << 20
WAITS = ()
BOTH = 0
WAVES = 1000


def polynomial(coefficients, s):
    value = coefficients[-1] * s + coefficients[-2]
    for c in coefficients[-3::-1]:
        value = value * s + c
    return value


def circle(turns):
    r = turns - jnp.round(turns)
    s = r * r
    return polynomial(COS, s), polynomial(SIN, s) * r


def tables(x, y, z, weight, put_x, put_y, put_z):
    c, s = circle(0.5 * x)
    twice = 4.0 * c * c - 2.0
    before, now = (c, -s), (c, s)
    for m in range(8):
        put_x(m, now[0])
        put_x(8 + m, now[1])
        before, now = now, tuple(twice * p - q for p, q in zip(now, before))
    c, s = circle(0.5 * y)
    twice = 4.0 * c * c - 2.0
    for l, value in enumerate((c, s, (twice - 1.0) * c, (twice + 1.0) * s)):
        put_y(l, value)
    c2 = 0.5 * twice * twice - 1.0
    s2 = 2.0 * twice * s * c
    four = 4.0 * c2 * c2
    for h, value in enumerate((c2, s2, c2 * (four - 3.0), s2 * (four - 1.0))):
        put_y(4 + h, value)
    real, imag = circle(8.5 * (x + y))
    c, s = circle(z)
    twice = c + c
    before, now = (weight, jnp.zeros_like(weight)), (weight * c, weight * s)
    for k in range(16):
        c, s = (value.astype(jnp.bfloat16).astype(jnp.float32) for value in now)
        put_z(k, real * c - imag * s)
        put_z(16 + k, real * s + imag * c)
        before, now = now, tuple(twice * p - q for p, q in zip(now, before))


def split(value):
    high = value.astype(jnp.bfloat16)
    return high, (value - high.astype(jnp.float32)).astype(jnp.bfloat16)


def slot_of(k):
    return jnp.where(k >= 9, k - 9, 16 - k)


def turned(value, quarter):
    return pltpu.roll(value, 64, 1) * quarter


def density_kernel(
    me_ref, wave_ref, length_ref, own_ref, sibling_ref, own_label, sibling_label, keep_ref, send_ref, *scratch, groups, bits, shift
):
    xs, ys, zs, prod, grid = scratch
    sources = ((own_ref, own_label), (sibling_ref, sibling_label))
    rows = own_ref.shape[0] // 3
    tiles = own_ref.shape[1] // 128

    def fill(g, source, j):
        ref, label_ref = sources[source]
        base = pl.multiple_of(g * 8, 8)
        lanes = pl.ds(pl.multiple_of(j * 128, 128), 128)
        x, y, z = (ref[pl.ds(base + rows * axis, 8), lanes] for axis in range(3))
        label = jnp.broadcast_to(label_ref[:, lanes], (8, 128))
        weight = jnp.zeros((8, 128), jnp.float32)
        for kind in range(length_ref.shape[0]):
            weight = weight + jnp.where(label == kind, length_ref[kind], 0.0)

        def put(table, pitch):
            def go(f, value):
                table[source * tiles + j, pl.ds(f, 8, stride=pitch), :] = value

            return go

        tables(x, y, z, weight, put(xs, PITCH), put(ys, PITCH), put(zs, WIDE))

    def one_frame(f, carry):
        r0 = f * PITCH
        total = jnp.zeros((128, 128), jnp.float32)
        for pair in range(tiles):
            left, right = [], []
            for t in (2 * pair, 2 * pair + 1):
                x = xs[t, pl.ds(r0, 16), :]
                z = zs[t, pl.ds(f * WIDE, 32), :]
                exact = jnp.concatenate([x * ys[t, pl.ds(r0 + l, 1), :] for l in range(4)], 0)
                left.append(jnp.concatenate(split(exact), 0))
                hs = [ys[t, pl.ds(r0 + 4 + h, 1), :] for h in range(4)]
                right.append(jnp.concatenate([part * h for part in (z[:16], z[16:]) for h in hs], 0).astype(jnp.bfloat16))
            total = total + lax.dot_general(
                jnp.concatenate(left, 1),
                jnp.concatenate(right, 1),
                (((1,), (1,)), ((), ())),
                preferred_element_type=jnp.float32,
            )
        prod[f] = total[:64] + total[64:]
        return carry

    def one_group(g, carry):
        for source in range(2):

            def one_tile(j, carry):
                fill(g, source, j)
                return carry

            lax.fori_loop(0, tiles, one_tile, 0, unroll=4)
        lax.fori_loop(0, 8, one_frame, 0, unroll=8)
        collect(g, me_ref, wave_ref, keep_ref, send_ref, prod, grid, bits, shift)
        return carry

    lax.fori_loop(0, groups, one_group, 0)


def collect(g, me_ref, wave_ref, keep_ref, send_ref, prod, grid, bits, shift):
    lane = lax.broadcasted_iota(jnp.int32, (8, 128), 1)
    quarter = jnp.where(lane < 64, -1.0, 1.0).astype(jnp.float32)
    for f in range(8):
        for l in range(4):
            cosine = prod[f, l * 16 : l * 16 + 8, :]
            sine = turned(prod[f, l * 16 + 8 : l * 16 + 16, :], quarter)
            r = (f * 4 + l) * PITCH
            grid[r : r + 8, :] = cosine + sine
            grid[r + 8 : r + 16, :] = cosine - sine

    me = me_ref[0]
    for i in range(8):
        flip = sum(((i >> (2 - j)) & 1) << bit for j, bit in enumerate(bits))
        pair = (me ^ flip) >> shift
        out_ref = keep_ref if i < 4 else send_ref
        for j in range(2):
            slot = slot_of(wave_ref[0, 2 * pair + j])
            for f in range(8):
                out_ref[g * 8 + f, i % 4, 4 * j : 4 * j + 4, :] = grid[pl.ds(f * 4 * PITCH + slot, 4, stride=PITCH), :]


def density(me, wave_numbers, lengths, own, sibling, own_label, sibling_label, groups, bits, shift):
    tiles = own.shape[1] // 128
    frames = groups * 8
    shape = jax.ShapeDtypeStruct((frames, 4, 8, 128), jnp.float32)
    smem, vmem = (pl.BlockSpec(memory_space=space) for space in (pltpu.SMEM, pltpu.VMEM))
    tables_shapes = [pltpu.VMEM((2 * tiles, 8 * pitch, 128), jnp.float32) for pitch in (PITCH, PITCH, WIDE)]
    return pl.pallas_call(
        functools.partial(density_kernel, groups=groups, bits=bits, shift=shift),
        out_shape=(shape, shape),
        in_specs=[smem] * 3 + [vmem] * 4,
        out_specs=(vmem, vmem),
        scratch_shapes=tables_shapes + [pltpu.VMEM((8, 64, 128), jnp.float32), pltpu.VMEM((32 * PITCH, 128), jnp.float32)],
        compiler_params=pltpu.CompilerParams(vmem_limit_bytes=VMEM_LIMIT),
        cost_estimate=pl.CostEstimate(flops=frames * tiles * 128 * 128 * 128 * 2 * 8, bytes_accessed=frames * 32768, transcendentals=0),
        name="density",
    )(me, wave_numbers, lengths, own, sibling, own_label, sibling_label)


def combine(value, swap, second, quarter):
    mixed = jnp.where(second, turned(value, quarter), value)
    return swap(mixed) + jnp.where(second, -mixed, mixed)


def waves_kernel(*refs, terms):
    parts, outs = refs[:terms], refs[terms:]
    frames = parts[0].shape[0]
    row = lax.broadcasted_iota(jnp.int32, (8, 128), 0)
    lane = lax.broadcasted_iota(jnp.int32, (8, 128), 1)
    quarter = jnp.where(lane < 64, -1.0, 1.0).astype(jnp.float32)
    bit_l, bit_h = (row & 1) == 1, (lane & 16) == 16

    def swap(axis, distance, second):
        size = (8, 128)[axis]

        def go(value):
            return jnp.where(second, pltpu.roll(value, distance, axis), pltpu.roll(value, size - distance, axis))

        return go

    for g, out in enumerate(outs):
        for t in range(frames):
            value = parts[0][t, g]
            for part in parts[1:]:
                value = value + part[t, g]
            value = combine(value, swap(0, 1, bit_l), bit_l, quarter)
            value = combine(value, swap(1, 16, bit_h), bit_h, quarter)
            out[:, t, :] = value


def waves(parts, groups):
    frames = parts[0].shape[0]
    shape = jax.ShapeDtypeStruct((8, frames, 128), jnp.float32)
    return pl.pallas_call(
        functools.partial(waves_kernel, terms=len(parts)),
        grid=(1,),
        out_shape=(shape,) * groups,
        in_specs=[pl.BlockSpec((frames, groups, 8, 128), lambda g: (0, 0, 0, 0))] * len(parts),
        out_specs=(pl.BlockSpec((8, frames, 128), lambda g: (0, 0, 0)),) * groups,
        compiler_params=pltpu.CompilerParams(vmem_limit_bytes=VMEM_LIMIT),
        name="waves",
    )(*parts)


def lags_kernel(place_ref, wave_ref, lag_ref, basis_ref, *refs, blocks, frames, atoms, period, share):
    parts, (out_ref, series, result) = refs[:blocks], refs[blocks:]
    half = period // 2
    tm, me = place_ref[0], place_ref[1]
    steps = blocks // len(RINGS)
    per_block = frames // steps
    at = 0
    for ring in range(len(RINGS)):
        size = parts[ring * steps].shape[2]
        for p in range(steps):
            for side in range(2):
                start = (tm ^ p) * per_block + ((me & 1) ^ side) * (per_block // 2) + at
                series[:, pl.ds(pl.multiple_of(start, 8), size), :] = parts[ring * steps + p][side]
        at += size
    lane = lax.broadcasted_iota(jnp.int32, (8, 128), 1)
    source = lane
    for n in range(16):
        source = jnp.where((lane & 15) == n, lane - n + wave_ref[2, n] - 1, source)
    count = lag_ref.shape[1]
    order = 2 * lax.broadcasted_iota(jnp.int32, (count, half), 1) + 1
    lag = jnp.broadcast_to(lag_ref[...], (half, count)).T
    phase = (order * lag).astype(jnp.float32)
    turns = phase - jnp.round(phase * (0.5 / period)) * (2.0 * period)
    cosine, _ = circle(turns * (0.5 / period))
    scale = (2.0 / period) / ((frames - lag).astype(jnp.float32) * float(atoms))
    high, low = split(cosine * scale)
    weights = jnp.concatenate([high, low, high], 1)
    powers = []
    for l in range(4):
        high, low = split(jnp.concatenate([series[l], series[4 + l]], 1))
        spectrum = jnp.dot(basis_ref[...], jnp.concatenate([high, high, low], 0), preferred_element_type=jnp.float32)
        power = spectrum[:half] * spectrum[:half] + spectrum[half:] * spectrum[half:]
        powers.append(
            jnp.concatenate(
                [
                    jnp.where(
                        lane < 64,
                        power[i : i + 8, :128] + pltpu.roll(power[i : i + 8, :128], 64, 1),
                        power[i : i + 8, 128:] + pltpu.roll(power[i : i + 8, 128:], 64, 1),
                    )
                    for i in range(0, half, 8)
                ],
                0,
            )
        )
    high, low = split(jnp.concatenate(powers, 1))
    total = jnp.dot(weights, jnp.concatenate([high, high, low], 0), preferred_element_type=jnp.float32)
    for l in range(4):
        part = total[:, l * 128 : l * 128 + 128]
        part = jnp.concatenate([jnp.take_along_axis(part[i : i + 8], source, axis=1) for i in range(0, count, 8)], 0)
        result[l] = part.T

    def place_of(b):
        k = wave_ref[1, b] - 1
        h, l = (jnp.where(v == 0, 3, jnp.where(v == 1, 1, jnp.where(v == 2, 0, 2))) for v in (k // 4, k % 4))
        return l, h * 16

    rows = share // 16
    known = [place_of(b) for b in range(16)] if rows == 32 else None
    for i in range(rows):
        if known:
            a, (l, start) = i // 16, known[i % 16]
        else:
            block = (me * rows + i) % 32
            a, (l, start) = block // 16, place_of(block % 16)
        out_ref[i * 16 : i * 16 + 16, :] = result[l, pl.ds(pl.multiple_of(a * 64 + start, 16), 16), :]


def lags(place, wave_numbers, lag_list, parts, frames, atoms, period, share):
    half = period // 2
    angle = np.outer(2 * np.arange(half) + 1, np.arange(frames)) * (math.pi / period)
    basis = np.concatenate([np.cos(angle), np.sin(angle)], 0).astype(np.float32)
    high = basis.astype(jnp.bfloat16)
    low = (basis - high.astype(np.float32)).astype(jnp.bfloat16)
    basis = jnp.asarray(np.concatenate([high, low, high], 1))
    smem = pl.BlockSpec(memory_space=pltpu.SMEM)
    vmem = pl.BlockSpec(memory_space=pltpu.VMEM)
    return pl.pallas_call(
        functools.partial(lags_kernel, blocks=len(parts), frames=frames, atoms=atoms, period=period, share=share),
        out_shape=jax.ShapeDtypeStruct((share, lag_list.shape[0]), jnp.float32),
        in_specs=[smem, smem] + [vmem] * (2 + len(parts)),
        out_specs=vmem,
        scratch_shapes=[pltpu.VMEM((8, frames, 128), jnp.float32), pltpu.VMEM((4, 128, lag_list.shape[0]), jnp.float32)],
        compiler_params=pltpu.CompilerParams(vmem_limit_bytes=VMEM_LIMIT),
        name="lags",
    )(place, wave_numbers, lag_list[None, :], basis, *parts)


def swapped(block, axis, flip):
    return lax.ppermute(block, axis, [(i, i ^ flip) for i in range(lax.axis_size(axis))])


def on_device(positions, species, lengths, wave_numbers, lag_list):
    frames, _, atoms = positions.shape
    devices, blocks = lax.axis_size("atom"), lax.axis_size("tm")
    me, tm = lax.axis_index("atom"), lax.axis_index("tm")
    share = wave_numbers.shape[1] ** 3 // devices
    period = (frames * blocks * 5) // 4
    half = frames // 2
    shift = devices.bit_length() - 4
    flips = [1 << bit for bit in range(1, devices.bit_length() - 1)]
    bits = ([bit for bit in range(1, devices.bit_length() - 1) if bit >= shift] + [0])[:3]

    turned_positions = jnp.transpose(positions, (1, 0, 2))
    sizes = [size * 8 for size in SIZES]

    def payload(core, start, size):
        part = lax.dynamic_slice_in_dim(turned_positions, core * half + start, size, 1)
        return part.reshape(3 * size, atoms)

    labels = [species[None, :], swapped(species, "atom", 1)[None, :]]
    place = jnp.stack([tm, me]).astype(jnp.int32)
    finals, rings, sums = [], [], []
    for c, size in enumerate(sizes):
        start = sum(sizes[:c])
        own = payload(me & 1, start, size)
        sibling = swapped(payload(1 - (me & 1), start, size), "atom", 1)
        sums.append(list(density(place[1:2], wave_numbers, lengths, own, sibling, *labels, size // 8, bits, shift)))
    held = [8] * len(sizes)
    terms = [[keep] for keep, _ in sums]
    for n, flip in enumerate(flips):
        for c in range(len(sizes)):
            if flip < (1 << shift):
                sums[c] = [a + swapped(a, "atom", flip) for a in sums[c]]
                terms[c] = sums[c][:1]
                continue
            held[c] //= 2
            out = sums[c][1] if held[c] == 4 else sum(t[:, held[c] : 2 * held[c]] for t in terms[c])
            terms[c].append(swapped(out, "atom", flip))
    for c, late, which in WAITS:
        terms[c][-1], terms[late][which] = lax.optimization_barrier((terms[c][-1], terms[late][which]))
    for c in range(len(sizes)):
        for chunk, ring in TIES:
            if chunk == c:
                terms[c][-1], *rings[ring][3:] = lax.optimization_barrier((terms[c][-1], *rings[ring][3:]))
        final = waves(terms[c], held[c])
        finals.append((final[0], final[-1]))
        for ring in RINGS:
            if ring[-1] == c:
                mine, other = (jnp.concatenate([finals[i][j] for i in ring], 1) for j in range(2))
                both = jnp.stack([mine, swapped(other, "atom", 1)])
                if c == 0 and BOTH:
                    both, terms[BOTH][1] = lax.optimization_barrier((both, terms[BOTH][1]))
                rings.append([both] + [swapped(both, "tm", p) for p in range(1, blocks)])
    parts = [part for ring in rings for part in ring]
    return lags(place, wave_numbers, lag_list, parts, frames * blocks, atoms * devices, period, share)


def solution(mesh):
    placed = (P("tm", None, "atom"), P("atom"), P(), P(), P())
    return jax.shard_map(
        on_device, mesh=mesh, in_specs=placed, out_specs=P("atom", None), check_vma=False
    )
```
